32 devices in a mesh: gz: 4 (over z), gy: 4 (over y, x), pa: 2 (over core).
Axes of the slice: x: 2, y: 2, z: 4, core: 2. Of those that a mesh axis runs over, the one named last changes fastest.
Arguments:
- probes: float32 [16, 32, 128, 512], P('pa', 'gz', 'gy'), may hold values from -40 to 40
- weight: float32 [32, 128, 512], P('gz', 'gy'), may hold values from 0.2 to 27
- courant: float32 [2, 3, 32, 128, 512], P(None, None, 'gz', 'gy'), may hold values from 0.03 to 0.3
- upwind_flags: int32 [2, 3, 32, 128, 512], P(None, None, 'gz', 'gy'), may hold values 0 or 1
Outputs:
- basis_rows: float32 [16, 32, 128, 512], P('pa', 'gz', 'gy')
- triangle: float32 [16, 16], replicated
The draws below stay inside these ranges and needn't reach their ends.
All inputs are finite; a program needn't handle non-finite values. No bound on the sum of `upwind_flags` on one device may be relied on, other than what follows from the above.
Results may differ from the reference program's by a relative error of at most 0.0002.
Values sent between devices are 32-bit elements; how exact they have to be, the bound alone decides.
A program may use at most 128 MiB of HBM per device.

```python
import math
import jax
import jax.numpy as jnp
from jax import lax

PROBES = 16
NX = 512
NZ = 32
NY = 128
CELLS = 2097152


def draw_probes(key, part):
    key_scale = jax.random.fold_in(key, 11)
    key_rough = jax.random.fold_in(key, 12)
    scales = jnp.exp(jax.random.uniform(key_scale, (PROBES, 1, 1, 1), jnp.float32, 0.0, math.log(10.0)))
    return scales * jax.random.truncated_normal(key_rough, -4.0, 4.0, (PROBES, NZ, NY, NX), jnp.float32)


def draw_weight(key, part):
    key_cells = jax.random.fold_in(key, 21)
    z_place = jnp.arange(NZ, dtype=jnp.float32)[:, None, None] / NZ
    rising = jnp.exp(math.log(3.0) * z_place)
    spread = jnp.exp(jax.random.uniform(key_cells, (NZ, NY, NX), jnp.float32, math.log(0.3), math.log(3.0)))
    return rising * spread


def set_ends(values, stream_key, smallest, top_value):
    extent = values.shape
    place = [jax.random.randint(jax.random.fold_in(stream_key, axis), (), 0, extent[axis]) for axis in range(len(extent))]
    values = values.at[tuple(place)].set(smallest)
    longest = extent.index(max(extent))
    place[longest] = (place[longest] + 1) % extent[longest]
    return values.at[tuple(place)].set(top_value)


def steps_of(stream_key, dims, cuts, low, largest):
    level = 1.0
    for position, blocks in cuts:
        heights = jax.random.uniform(jax.random.fold_in(jax.random.fold_in(stream_key, 6), position), (blocks,), jnp.float32, low / len(cuts), largest / len(cuts))
        level = level * jnp.repeat(jnp.exp(heights), dims[position] // blocks).reshape((-1,) + (1,) * (len(dims) - 1 - position))
    return level


def setup_inputs(seed: int = 0) -> dict:
    splits = jax.random.split(jax.random.key(seed), 5)
    return {
        "probes": draw_probes(jax.random.fold_in(splits[4], 71), 0),
        "weight": draw_weight(jax.random.fold_in(splits[4], 71), 0),
        "courant": jnp.clip(jnp.exp(math.log(0.3) - 2.3025852 * jax.random.uniform(splits[2], (2, 3, NZ, NY, NX), jnp.float32) ** steps_of(splits[2], (2, 3, NZ, NY, NX), ((2, 4), (3, 4)), -0.2, 0.2)), 0.03, 0.3),
        "upwind_flags": set_ends((jax.random.randint(splits[3], (2, 3, NZ, NY, NX), 0, 2) < 1).astype(jnp.int32), jax.random.fold_in(splits[3], 1), 0, 1),
    }


def advance(extended, courant_now, from_below):
    centre = extended[:, 1:-1, 1:-1, 1:-1]
    below_z = extended[:, :-2, 1:-1, 1:-1]
    above_z = extended[:, 2:, 1:-1, 1:-1]
    below_y = extended[:, 1:-1, :-2, 1:-1]
    above_y = extended[:, 1:-1, 2:, 1:-1]
    below_x = extended[:, 1:-1, 1:-1, :-2]
    above_x = extended[:, 1:-1, 1:-1, 2:]
    summed = courant_now[0] * (centre - jnp.where(from_below[0], below_z, above_z))
    summed = summed + courant_now[1] * (centre - jnp.where(from_below[1], below_y, above_y))
    summed = summed + courant_now[2] * (centre - jnp.where(from_below[2], below_x, above_x))
    return centre - summed

def factor_gram(gram_total):
    order = gram_total.shape[0]
    places = jnp.arange(order, dtype=jnp.int32)
    lower = jnp.zeros((order, order), jnp.float32)
    for column in range(order):
        known = lax.optimization_barrier(jnp.sum(lower * lower[column][None, :], axis=1))
        remain = gram_total[:, column] - known
        pivot = jnp.sqrt(remain[column])
        filled = jnp.where(places > column, remain / pivot, jnp.where(places == column, pivot, 0.0))
        lower = lower + filled[:, None] * (places == column).astype(jnp.float32)[None, :]
    solved = jnp.zeros((order, order), jnp.float32)
    for row_number in range(order):
        unit_row = (places == row_number).astype(jnp.float32)
        carried = lax.optimization_barrier(jnp.sum(lower[row_number][:, None] * solved, axis=0))
        new_row = (unit_row - carried) / lower[row_number, row_number]
        solved = solved + unit_row[:, None] * new_row[None, :]
    return (lower.T, solved.T)

def reference(probes, weight, courant, upwind_flags):

    def one_probe(single):
        density = single[None]
        for number in range(2):
            padded = jnp.pad(density, ((0, 0), (1, 1), (1, 1), (1, 1)))
            density = advance(padded, courant[number], upwind_flags[number] == 1)
        return weight * density[0]
    sketch = lax.map(one_probe, probes)
    flat_rows = sketch.reshape(PROBES, -1)
    gram_total = jnp.dot(flat_rows, flat_rows.T, precision=lax.Precision.HIGHEST) / CELLS
    triangle, inverse = factor_gram(gram_total)
    basis_rows = jnp.dot(inverse.T, flat_rows, precision=lax.Precision.HIGHEST)
    return (basis_rows.reshape(PROBES, NZ, NY, NX), triangle)
```

```python
import functools

import jax
import jax.numpy as jnp
from jax import lax
from jax.experimental import pallas as pl
from jax.experimental.pallas import tpu as pltpu
from jax.sharding import PartitionSpec as P

MESH = pl.DeviceIdType.MESH
HIGHEST = lax.Precision.HIGHEST
GROUP = 2
PAD = 8


def sketch_kernel(sizes, probes, weight, courant, flags, y_own, y_part, fact,
                  u0, u1, own, part, cbuf, fbuf, wbuf, centre, gacc, pairs, g_send, g_recv, s_send, s_recv,
                  load_sems, zs_send, zs_recv, ys_send, ys_recv, ps_send, ps_recv,
                  out_sems, a_send, a_recv, b_send, b_recv):
    n_gz, n_gy, n_pa = sizes
    count, planes, rows, width = probes.shape
    groups = count // GROUP
    tiles = rows // 8
    gz, gy, pa = lax.axis_index("gz"), lax.axis_index("gy"), lax.axis_index("pa")
    body = pl.ds(PAD, rows)
    inner = pl.ds(1, planes)

    loads = [
        pltpu.make_async_copy(probes, u0.at[:, inner, body, :], load_sems.at[0]),
        pltpu.make_async_copy(courant, cbuf, load_sems.at[1]),
        pltpu.make_async_copy(flags, fbuf, load_sems.at[2]),
        pltpu.make_async_copy(weight, wbuf, load_sems.at[3]),
    ]
    for load in loads:
        load.start()

    team = n_gy * n_pa
    place = gy * n_pa + pa

    def team_peer(offset):
        other = lax.rem(place + offset, team)
        return {"gy": other // n_pa, "pa": lax.rem(other, n_pa)}

    def column_peer(offset):
        return {"gz": lax.rem(gz + offset, n_gz)}

    barrier = pltpu.get_barrier_semaphore()
    for offset in range(1, team):
        pl.semaphore_signal(barrier, inc=1, device_id=team_peer(offset), device_id_type=MESH)
    for offset in range(1, n_gz):
        pl.semaphore_signal(barrier, inc=1, device_id=column_peer(offset), device_id_type=MESH)
    pl.semaphore_wait(barrier, team + n_gz - 2)

    has_next = (gz < n_gz - 1, gy < n_gy - 1)
    has_before = (gz > 0, gy > 0)

    def z_copy(phase, direction, group):
        picked = pl.ds(group * GROUP, GROUP)
        source_plane = planes - 1 if direction == 0 else 0
        target_plane = 0 if direction == 0 else planes + 1
        if phase == 0:
            source = probes.at[picked, source_plane]
        else:
            source = u1.at[picked, source_plane + 1, body, :]
        target = (u0, u1)[phase].at[picked, target_plane, body, :]
        step = 1 if direction == 0 else n_gz - 1
        return pltpu.make_async_remote_copy(
            src_ref=source, dst_ref=target,
            send_sem=zs_send.at[phase, direction, group], recv_sem=zs_recv.at[phase, direction, group],
            device_id={"gz": lax.rem(gz + step, n_gz)}, device_id_type=MESH)

    def y_copy(phase, direction):
        source_row = rows - 1 if direction == 0 else 0
        target_row = PAD - 1 if direction == 0 else PAD + rows
        if phase == 0:
            source = probes.at[:, :, pl.ds(source_row, 1), :]
        else:
            source = u1.at[:, inner, pl.ds(source_row + PAD, 1), :]
        target = (u0, u1)[phase].at[:, inner, pl.ds(target_row, 1), :]
        step = 1 if direction == 0 else n_gy - 1
        return pltpu.make_async_remote_copy(
            src_ref=source, dst_ref=target,
            send_sem=ys_send.at[phase, direction], recv_sem=ys_recv.at[phase, direction],
            device_id={"gy": lax.rem(gy + step, n_gy)}, device_id_type=MESH)

    def started(axis, direction):
        return has_next[axis] if direction == 0 else has_before[axis]

    def awaited(axis, direction):
        return has_before[axis] if direction == 0 else has_next[axis]

    def start_z(phase, group):
        for direction in range(2):
            @pl.when(started(0, direction))
            def _():
                z_copy(phase, direction, group).start()

    def wait_z(phase, group):
        for direction in range(2):
            @pl.when(awaited(0, direction))
            def _():
                z_copy(phase, direction, group).wait_recv()

    def start_y(phase):
        for direction in range(2):
            @pl.when(started(1, direction))
            def _():
                y_copy(phase, direction).start()

    def wait_y(phase):
        for direction in range(2):
            @pl.when(awaited(1, direction))
            def _():
                y_copy(phase, direction).wait_recv()

    start_y(0)
    for group in range(groups):
        start_z(0, group)

    for buffer in (u0, u1):
        for direction in range(2):
            plane = 0 if direction == 0 else planes + 1
            row = PAD - 1 if direction == 0 else PAD + rows

            @pl.when(jnp.logical_not(awaited(0, direction)))
            def _():
                def clear(k, carry):
                    buffer[k, plane, PAD:PAD + rows, :] = jnp.zeros((rows, width), jnp.float32)
                    return carry
                lax.fori_loop(0, count, clear, 0)

            @pl.when(jnp.logical_not(awaited(1, direction)))
            def _():
                def clear(i, carry):
                    buffer[i // planes, 1 + lax.rem(i, planes), row:row + 1, :] = jnp.zeros((1, width), jnp.float32)
                    return carry
                lax.fori_loop(0, count * planes, clear, 0)

    loads[1].wait()
    loads[2].wait()
    lane = lax.broadcasted_iota(jnp.int32, (rows, width), 1)

    def prepare(i, carry):
        s, z = i // planes, lax.rem(i, planes)
        cx = cbuf[s, 2, z]
        centre[s, z] = 1.0 - (cbuf[s, 0, z] + cbuf[s, 1, z] + cx)
        edge = jnp.where(fbuf[s, 2, z] == 1, 0, width - 1)
        cbuf[s, 2, z] = jnp.where(lane == edge, 0.0, cx)
        return carry

    lax.fori_loop(0, 2 * planes, prepare, 0)

    def advance(source, s, z, first, store):
        for tile in range(tiles):
            low = tile * 8
            here = (slice(low, low + 8), slice(None))
            c0 = centre[(s, z) + here]
            cz, cy, cx = (cbuf[(s, d, z) + here] for d in range(3))
            fz, fy, fx = (fbuf[(s, d, z) + here] == 1 for d in range(3))
            at = PAD + low
            for k in range(GROUP):
                number = first + k
                u = source[number, z + 1, at:at + 8, :]
                n_z = jnp.where(fz, source[number, z, at:at + 8, :], source[number, z + 2, at:at + 8, :])
                n_y = jnp.where(fy, source[number, z + 1, at - 1:at + 7, :], source[number, z + 1, at + 1:at + 9, :])
                n_x = jnp.where(fx, pltpu.roll(u, 1, 1), pltpu.roll(u, width - 1, 1))
                store(number, z, low, c0 * u + cz * n_z + cy * n_y + cx * n_x)

    def store_first(number, z, low, value):
        u1[number, z + 1, PAD + low:PAD + low + 8, :] = value

    def store_sketch(number, z, low, value):
        own[number, z, low:low + 8, :] = wbuf[z, low:low + 8, :] * value

    def sweep_inner(source, s, store):
        def step(i, carry):
            advance(source, s, 1 + i // groups, lax.rem(i, groups) * GROUP, store)
            return carry
        lax.fori_loop(0, (planes - 2) * groups, step, 0)

    def sweep_edges(source, s, group, store):
        def step(i, carry):
            advance(source, s, i * (planes - 1), group * GROUP, store)
            return carry
        lax.fori_loop(0, 2, step, 0)

    loads[0].wait()
    loads[3].wait()
    wait_y(0)
    sweep_inner(u0, 0, store_first)
    for group in range(groups):
        wait_z(0, group)
        sweep_edges(u0, 0, group, store_first)
        start_z(1, group)
    start_y(1)
    wait_y(1)
    sweep_inner(u1, 1, store_sketch)

    def edge_copy(group, side):
        picked = (pl.ds(group * GROUP, GROUP), side * (planes - 1))
        index = 1 + 2 * group + side
        return pltpu.make_async_remote_copy(
            src_ref=own.at[picked], dst_ref=part.at[picked],
            send_sem=ps_send.at[index], recv_sem=ps_recv.at[index],
            device_id={"pa": lax.rem(pa + 1, n_pa)}, device_id_type=MESH)

    bulk = pl.ds(1, planes - 2)
    bulk_copy = pltpu.make_async_remote_copy(
        src_ref=own.at[:, bulk], dst_ref=part.at[:, bulk],
        send_sem=ps_send.at[0], recv_sem=ps_recv.at[0],
        device_id={"pa": lax.rem(pa + 1, n_pa)}, device_id_type=MESH)
    bulk_copy.start()
    stores = [pltpu.make_async_copy(own.at[:, bulk], y_own.at[:, bulk], out_sems.at[0])]
    stores[0].start()

    total = 2 * count
    half = count // 2
    blocks = [
        [(a, b) for a in range(count) for b in range(a, count)],
        [(a, b) for a in range(count, total) for b in range(a, total)],
        [(a, b) for a in range(half) for b in range(count, total)],
        [(a, b) for a in range(half, count) for b in range(count, total)],
    ]

    def products(first_plane, plane_count, begin):
        for block in blocks:
            used = sorted({i for pair in block for i in pair})

            def step(i, sums, block=block, used=used):
                z = first_plane + i // tiles
                at = pl.ds(pl.multiple_of(lax.rem(i, tiles) * 8, 8), 8)
                sums = list(sums)
                for piece in range(width // 128):
                    cells = slice(piece * 128, piece * 128 + 128)
                    rows_now = {}
                    for n in used:
                        holder = own if n < count else part
                        rows_now[n] = holder[n % count, z, at, cells]
                    for spot, (a, b) in enumerate(block):
                        sums[spot] = sums[spot] + rows_now[a] * rows_now[b]
                return tuple(sums)

            if begin:
                sums = tuple(jnp.zeros((8, 128), jnp.float32) for _ in block)
            else:
                sums = tuple(gacc[a * total + b] for a, b in block)
            sums = lax.fori_loop(0, plane_count * tiles, step, sums)
            for (a, b), value in zip(block, sums):
                if begin:
                    gacc[a * total + b] = value
                else:
                    line = jnp.sum(value, axis=0, keepdims=True)
                    pairs[a * total + b:a * total + b + 1, :] = line
                    if a != b:
                        pairs[b * total + a:b * total + a + 1, :] = line

    bulk_copy.wait_recv()
    stores.append(pltpu.make_async_copy(part.at[:, bulk], y_part.at[:, bulk], out_sems.at[1]))
    stores[1].start()
    quarter = planes // 2 - 1
    products(1 + quarter * pa, quarter, True)

    for group in range(groups):
        wait_z(1, group)
        sweep_edges(u1, 1, group, store_sketch)
        for side in range(2):
            edge_copy(group, side).start()
    for side in range(2):
        plane = side * (planes - 1)
        stores.append(pltpu.make_async_copy(own.at[:, plane], y_own.at[:, plane], out_sems.at[2 + side]))
        stores[-1].start()
    for group in range(groups):
        for side in range(2):
            edge_copy(group, side).wait_recv()
    for side in range(2):
        plane = side * (planes - 1)
        stores.append(pltpu.make_async_copy(part.at[:, plane], y_part.at[:, plane], out_sems.at[4 + side]))
        stores[-1].start()
    products((planes - 1) * pa, 1, False)

    flip = pa * count
    entries = total * total
    summed = lax.dot_general(jnp.ones((8, 128), jnp.float32), pairs[...], (((1,), (1,)), ((), ())),
                             precision=HIGHEST, preferred_element_type=jnp.float32)
    spread_row = lax.broadcasted_iota(jnp.int32, (total, entries), 0)
    spread_col = lax.broadcasted_iota(jnp.int32, (total, entries), 1)
    picked_row = lax.rem(spread_row + flip, total) == spread_col // total
    spread = jnp.where(picked_row, jnp.broadcast_to(summed[0:1, :], (total, entries)), 0.0)
    gather_row = lax.broadcasted_iota(jnp.int32, (entries, 128), 0)
    gather_col = lax.broadcasted_iota(jnp.int32, (entries, 128), 1)
    gather = (lax.rem(gather_row, total) == lax.rem(gather_col + flip, total)) & (gather_col < total)
    gram = jnp.dot(spread, gather.astype(jnp.float32), precision=HIGHEST, preferred_element_type=jnp.float32)

    def spread_sum(value, sender, receiver, mine, peers, peer_of, send_sems, recv_sems):
        sender[...] = value
        receiver[mine] = value
        for offset in range(1, peers):
            pltpu.make_async_remote_copy(
                src_ref=sender, dst_ref=receiver.at[mine],
                send_sem=send_sems.at[offset - 1], recv_sem=recv_sems.at[offset - 1],
                device_id=peer_of(offset), device_id_type=MESH).start()
        for offset in range(1, peers):
            origin = lax.rem(mine + peers - offset, peers)
            pltpu.make_async_remote_copy(
                src_ref=sender, dst_ref=receiver.at[origin],
                send_sem=send_sems.at[offset - 1], recv_sem=recv_sems.at[offset - 1],
                device_id=peer_of(offset), device_id_type=MESH).wait_recv()
        result = receiver[0]
        for n in range(1, peers):
            result = result + receiver[n]
        return result

    gram = spread_sum(gram, g_send, g_recv, place, team, team_peer, a_send, a_recv)
    gram = spread_sum(gram, s_send, s_recv, gz, n_gz, column_peer, b_send, b_recv)
    gram = gram * (1.0 / (planes * rows * width * n_gz * n_gy))

    line = lax.broadcasted_iota(jnp.int32, (total, 128), 0)
    column = lax.broadcasted_iota(jnp.int32, (total, 128), 1)
    system = gram + jnp.where(column == line + total, 1.0, 0.0)
    scaled = jnp.zeros_like(system)
    for c in range(total):
        row = jnp.broadcast_to(system[c:c + 1, :], (total, 128))
        factor = jnp.broadcast_to(system[:, c:c + 1], (total, 128))
        pivot = jnp.broadcast_to(factor[c:c + 1, :], (total, 128))
        scaled = jnp.where(line == c, system / jnp.sqrt(pivot), scaled)
        if c < total - 1:
            system = jnp.where(line > c, system - (factor / pivot) * row, system)
    fact[...] = jnp.where((column < line), 0.0, scaled)

    for store in stores:
        store.wait()
    for phase in range(2):
        for direction in range(2):
            @pl.when(started(0, direction))
            def _():
                for group in range(groups):
                    z_copy(phase, direction, group).wait_send()

            @pl.when(started(1, direction))
            def _():
                y_copy(phase, direction).wait_send()
    bulk_copy.wait_send()
    for group in range(groups):
        for side in range(2):
            edge_copy(group, side).wait_send()
    for peers, sender, receiver, peer_of, send_sems, recv_sems in (
            (team, g_send, g_recv, team_peer, a_send, a_recv),
            (n_gz, s_send, s_recv, column_peer, b_send, b_recv)):
        for offset in range(1, peers):
            pltpu.make_async_remote_copy(
                src_ref=sender, dst_ref=receiver.at[0],
                send_sem=send_sems.at[offset - 1], recv_sem=recv_sems.at[offset - 1],
                device_id=peer_of(offset), device_id_type=MESH).wait_send()


def basis_kernel(scalars, fact, own, part, basis, triangle):
    count, _, rows, _ = own.shape
    total = 2 * count
    pa = lax.axis_index("pa")
    triangle[...] = fact[:, :total]
    first, other = pa * count, (1 - pa) * count

    def step(i, carry):
        at = pl.ds(pl.multiple_of(i * 8, 8), 8)
        for k in range(count):
            value = scalars[first + k, total + first] * own[0, 0, at, :]
            for j in range(1, count):
                value = value + scalars[first + k, total + first + j] * own[j, 0, at, :]
            for j in range(count):
                value = value + scalars[first + k, total + other + j] * part[j, 0, at, :]
            basis[k, 0, at, :] = value
        return carry

    lax.fori_loop(0, rows // 8, step, 0)


def shards(probes, weight, courant, upwind_flags):
    count, planes, rows, width = probes.shape
    sizes = tuple(lax.axis_size(axis) for axis in ("gz", "gy", "pa"))
    n_gz, n_gy, n_pa = sizes
    total = 2 * count
    team = n_gy * n_pa
    groups = count // GROUP
    f32 = jnp.float32
    dma = pltpu.SemaphoreType.DMA
    anywhere = pl.BlockSpec(memory_space=pl.ANY)
    y_own, y_part, fact = pl.pallas_call(
        functools.partial(sketch_kernel, sizes),
        out_shape=(
            jax.ShapeDtypeStruct(probes.shape, f32),
            jax.ShapeDtypeStruct(probes.shape, f32),
            jax.ShapeDtypeStruct((total, 128), f32),
        ),
        in_specs=[anywhere] * 4,
        out_specs=(anywhere, anywhere, pl.BlockSpec(memory_space=pltpu.VMEM)),
        scratch_shapes=[
            pltpu.VMEM((count, planes + 2, rows + 2 * PAD, width), f32),
            pltpu.VMEM((count, planes + 2, rows + 2 * PAD, width), f32),
            pltpu.VMEM(probes.shape, f32),
            pltpu.VMEM(probes.shape, f32),
            pltpu.VMEM(courant.shape, f32),
            pltpu.VMEM(upwind_flags.shape, jnp.int32),
            pltpu.VMEM(weight.shape, f32),
            pltpu.VMEM((2, planes, rows, width), f32),
            pltpu.VMEM((total * total, 8, 128), f32),
            pltpu.VMEM((total * total, 128), f32),
            pltpu.VMEM((total, 128), f32),
            pltpu.VMEM((team, total, 128), f32),
            pltpu.VMEM((total, 128), f32),
            pltpu.VMEM((n_gz, total, 128), f32),
            dma((4,)),
            dma((2, 2, groups)),
            dma((2, 2, groups)),
            dma((2, 2)),
            dma((2, 2)),
            dma((1 + 2 * groups,)),
            dma((1 + 2 * groups,)),
            dma((6,)),
            dma((team,)),
            dma((team,)),
            dma((n_gz,)),
            dma((n_gz,)),
        ],
        compiler_params=pltpu.CompilerParams(
            collective_id=0, has_side_effects=True, vmem_limit_bytes=52 * 1024 * 1024),
        name="sketch",
    )(probes, weight, courant, upwind_flags)
    block = pl.BlockSpec((count, 1, rows, width), lambda z: (0, z, 0, 0))
    return pl.pallas_call(
        basis_kernel,
        grid=(planes,),
        out_shape=(
            jax.ShapeDtypeStruct(probes.shape, f32),
            jax.ShapeDtypeStruct((total, total), f32),
        ),
        in_specs=[
            pl.BlockSpec(memory_space=pltpu.SMEM),
            pl.BlockSpec((total, 128), lambda z: (0, 0)),
            block,
            block,
        ],
        out_specs=(block, pl.BlockSpec((total, total), lambda z: (0, 0))),
        compiler_params=pltpu.CompilerParams(vmem_limit_bytes=16 * 1024 * 1024),
        name="basis",
    )(fact, fact, y_own, y_part)


def solution(mesh):
    placed = (
        P("pa", "gz", "gy", None),
        P("gz", "gy", None),
        P(None, None, "gz", "gy", None),
        P(None, None, "gz", "gy", None),
    )
    return jax.shard_map(
        shards,
        mesh=mesh,
        in_specs=placed,
        out_specs=(P("pa", "gz", "gy", None), P()),
        check_vma=False,
    )
```

```python
import functools

import jax
import jax.numpy as jnp
from jax import lax
from jax.experimental import pallas as pl
from jax.experimental.pallas import tpu as pltpu
from jax.sharding import PartitionSpec as P

MESH = pl.DeviceIdType.MESH
HIGHEST = lax.Precision.HIGHEST
GROUP = 2
PAD = 8


def sketch_kernel(sizes, probes, weight, courant, flags, own, part, fact,
                  u0, u1, cbuf, fbuf, wbuf, centre, gacc, pairs, g_send, g_recv, s_send, s_recv,
                  load_sems, zs_send, zs_recv, ys_send, ys_recv, ps_send, ps_recv,
                  a_send, a_recv, b_send, b_recv):
    n_gz, n_gy, n_pa = sizes
    count, planes, rows, width = probes.shape
    groups = count // GROUP
    tiles = rows // 8
    gz, gy, pa = lax.axis_index("gz"), lax.axis_index("gy"), lax.axis_index("pa")
    body = pl.ds(PAD, rows)
    inner = pl.ds(1, planes)

    loads = [
        pltpu.make_async_copy(probes, u0.at[:, inner, body, :], load_sems.at[0]),
        pltpu.make_async_copy(courant, cbuf, load_sems.at[1]),
        pltpu.make_async_copy(flags, fbuf, load_sems.at[2]),
        pltpu.make_async_copy(weight, wbuf, load_sems.at[3]),
    ]
    for load in loads:
        load.start()

    team = n_gy * n_pa
    place = gy * n_pa + pa

    def team_peer(offset):
        other = lax.rem(place + offset, team)
        return {"gy": other // n_pa, "pa": lax.rem(other, n_pa)}

    def column_peer(offset):
        return {"gz": lax.rem(gz + offset, n_gz)}

    barrier = pltpu.get_barrier_semaphore()
    for offset in range(1, team):
        pl.semaphore_signal(barrier, inc=1, device_id=team_peer(offset), device_id_type=MESH)
    for offset in range(1, n_gz):
        pl.semaphore_signal(barrier, inc=1, device_id=column_peer(offset), device_id_type=MESH)
    pl.semaphore_wait(barrier, team + n_gz - 2)

    has_next = (gz < n_gz - 1, gy < n_gy - 1)
    has_before = (gz > 0, gy > 0)

    def z_copy(phase, direction, group):
        picked = pl.ds(group * GROUP, GROUP)
        source_plane = planes - 1 if direction == 0 else 0
        target_plane = 0 if direction == 0 else planes + 1
        if phase == 0:
            source = probes.at[picked, source_plane]
        else:
            source = u1.at[picked, source_plane + 1, body, :]
        target = (u0, u1)[phase].at[picked, target_plane, body, :]
        step = 1 if direction == 0 else n_gz - 1
        return pltpu.make_async_remote_copy(
            src_ref=source, dst_ref=target,
            send_sem=zs_send.at[phase, direction, group], recv_sem=zs_recv.at[phase, direction, group],
            device_id={"gz": lax.rem(gz + step, n_gz)}, device_id_type=MESH)

    def y_copy(phase, direction):
        source_row = rows - 1 if direction == 0 else 0
        target_row = PAD - 1 if direction == 0 else PAD + rows
        if phase == 0:
            source = probes.at[:, :, pl.ds(source_row, 1), :]
        else:
            source = u1.at[:, inner, pl.ds(source_row + PAD, 1), :]
        target = (u0, u1)[phase].at[:, inner, pl.ds(target_row, 1), :]
        step = 1 if direction == 0 else n_gy - 1
        return pltpu.make_async_remote_copy(
            src_ref=source, dst_ref=target,
            send_sem=ys_send.at[phase, direction], recv_sem=ys_recv.at[phase, direction],
            device_id={"gy": lax.rem(gy + step, n_gy)}, device_id_type=MESH)

    def started(axis, direction):
        return has_next[axis] if direction == 0 else has_before[axis]

    def awaited(axis, direction):
        return has_before[axis] if direction == 0 else has_next[axis]

    def start_z(phase, group):
        for direction in range(2):
            @pl.when(started(0, direction))
            def _():
                z_copy(phase, direction, group).start()

    def wait_z(phase, group):
        for direction in range(2):
            @pl.when(awaited(0, direction))
            def _():
                z_copy(phase, direction, group).wait_recv()

    def start_y(phase):
        for direction in range(2):
            @pl.when(started(1, direction))
            def _():
                y_copy(phase, direction).start()

    def wait_y(phase):
        for direction in range(2):
            @pl.when(awaited(1, direction))
            def _():
                y_copy(phase, direction).wait_recv()

    start_y(0)
    for group in range(groups):
        start_z(0, group)

    for buffer in (u0, u1):
        for direction in range(2):
            plane = 0 if direction == 0 else planes + 1
            row = PAD - 1 if direction == 0 else PAD + rows

            @pl.when(jnp.logical_not(awaited(0, direction)))
            def _():
                def clear(k, carry):
                    buffer[k, plane, PAD:PAD + rows, :] = jnp.zeros((rows, width), jnp.float32)
                    return carry
                lax.fori_loop(0, count, clear, 0)

            @pl.when(jnp.logical_not(awaited(1, direction)))
            def _():
                def clear(i, carry):
                    buffer[i // planes, 1 + lax.rem(i, planes), row:row + 1, :] = jnp.zeros((1, width), jnp.float32)
                    return carry
                lax.fori_loop(0, count * planes, clear, 0)

    loads[1].wait()
    loads[2].wait()
    lane = lax.broadcasted_iota(jnp.int32, (rows, width), 1)

    def prepare(i, carry):
        s, z = i // planes, lax.rem(i, planes)
        cx = cbuf[s, 2, z]
        centre[s, z] = 1.0 - (cbuf[s, 0, z] + cbuf[s, 1, z] + cx)
        edge = jnp.where(fbuf[s, 2, z] == 1, 0, width - 1)
        cbuf[s, 2, z] = jnp.where(lane == edge, 0.0, cx)
        return carry

    lax.fori_loop(0, 2 * planes, prepare, 0)

    def advance(source, s, z, first, store):
        for tile in range(tiles):
            low = tile * 8
            here = (slice(low, low + 8), slice(None))
            c0 = centre[(s, z) + here]
            cz, cy, cx = (cbuf[(s, d, z) + here] for d in range(3))
            fz, fy, fx = (fbuf[(s, d, z) + here] == 1 for d in range(3))
            at = PAD + low
            for k in range(GROUP):
                number = first + k
                u = source[number, z + 1, at:at + 8, :]
                n_z = jnp.where(fz, source[number, z, at:at + 8, :], source[number, z + 2, at:at + 8, :])
                n_y = jnp.where(fy, source[number, z + 1, at - 1:at + 7, :], source[number, z + 1, at + 1:at + 9, :])
                n_x = jnp.where(fx, pltpu.roll(u, 1, 1), pltpu.roll(u, width - 1, 1))
                store(number, z, low, c0 * u + cz * n_z + cy * n_y + cx * n_x)

    def store_first(number, z, low, value):
        u1[number, z + 1, PAD + low:PAD + low + 8, :] = value

    def store_sketch(number, z, low, value):
        own[number, z, low:low + 8, :] = wbuf[z, low:low + 8, :] * value

    def sweep_inner(source, s, store):
        def step(i, carry):
            advance(source, s, 1 + i // groups, lax.rem(i, groups) * GROUP, store)
            return carry
        lax.fori_loop(0, (planes - 2) * groups, step, 0)

    def sweep_edges(source, s, group, store):
        def step(i, carry):
            advance(source, s, i * (planes - 1), group * GROUP, store)
            return carry
        lax.fori_loop(0, 2, step, 0)

    loads[0].wait()
    loads[3].wait()
    wait_y(0)
    sweep_inner(u0, 0, store_first)
    for group in range(groups):
        wait_z(0, group)
        sweep_edges(u0, 0, group, store_first)
        start_z(1, group)
    start_y(1)
    wait_y(1)
    sweep_inner(u1, 1, store_sketch)

    def edge_copy(group, side):
        picked = (pl.ds(group * GROUP, GROUP), side * (planes - 1))
        index = 1 + 2 * group + side
        return pltpu.make_async_remote_copy(
            src_ref=own.at[picked], dst_ref=part.at[picked],
            send_sem=ps_send.at[index], recv_sem=ps_recv.at[index],
            device_id={"pa": lax.rem(pa + 1, n_pa)}, device_id_type=MESH)

    bulk = pl.ds(1, planes - 2)
    bulk_copy = pltpu.make_async_remote_copy(
        src_ref=own.at[:, bulk], dst_ref=part.at[:, bulk],
        send_sem=ps_send.at[0], recv_sem=ps_recv.at[0],
        device_id={"pa": lax.rem(pa + 1, n_pa)}, device_id_type=MESH)
    bulk_copy.start()

    total = 2 * count
    half = count // 2
    blocks = [
        [(a, b) for a in range(count) for b in range(a, count)],
        [(a, b) for a in range(count, total) for b in range(a, total)],
        [(a, b) for a in range(half) for b in range(count, total)],
        [(a, b) for a in range(half, count) for b in range(count, total)],
    ]

    def products(first_plane, plane_count, begin):
        for block in blocks:
            used = sorted({i for pair in block for i in pair})

            def step(i, sums, block=block, used=used):
                z = first_plane + i // tiles
                at = pl.ds(pl.multiple_of(lax.rem(i, tiles) * 8, 8), 8)
                sums = list(sums)
                for piece in range(width // 128):
                    cells = slice(piece * 128, piece * 128 + 128)
                    rows_now = {}
                    for n in used:
                        holder = own if n < count else part
                        rows_now[n] = holder[n % count, z, at, cells]
                    for spot, (a, b) in enumerate(block):
                        sums[spot] = sums[spot] + rows_now[a] * rows_now[b]
                return tuple(sums)

            if begin:
                sums = tuple(jnp.zeros((8, 128), jnp.float32) for _ in block)
            else:
                sums = tuple(gacc[a * total + b] for a, b in block)
            sums = lax.fori_loop(0, plane_count * tiles, step, sums)
            for (a, b), value in zip(block, sums):
                if begin:
                    gacc[a * total + b] = value
                else:
                    line = jnp.sum(value, axis=0, keepdims=True)
                    pairs[a * total + b:a * total + b + 1, :] = line
                    if a != b:
                        pairs[b * total + a:b * total + a + 1, :] = line

    bulk_copy.wait_recv()
    quarter = planes // 2 - 1
    products(1 + quarter * pa, quarter, True)

    for group in range(groups):
        wait_z(1, group)
        sweep_edges(u1, 1, group, store_sketch)
        for side in range(2):
            edge_copy(group, side).start()
    for group in range(groups):
        for side in range(2):
            edge_copy(group, side).wait_recv()
    products((planes - 1) * pa, 1, False)

    flip = pa * count
    entries = total * total
    summed = lax.dot_general(jnp.ones((8, 128), jnp.float32), pairs[...], (((1,), (1,)), ((), ())),
                             precision=HIGHEST, preferred_element_type=jnp.float32)
    spread_row = lax.broadcasted_iota(jnp.int32, (total, entries), 0)
    spread_col = lax.broadcasted_iota(jnp.int32, (total, entries), 1)
    picked_row = lax.rem(spread_row + flip, total) == spread_col // total
    spread = jnp.where(picked_row, jnp.broadcast_to(summed[0:1, :], (total, entries)), 0.0)
    gather_row = lax.broadcasted_iota(jnp.int32, (entries, 128), 0)
    gather_col = lax.broadcasted_iota(jnp.int32, (entries, 128), 1)
    gather = (lax.rem(gather_row, total) == lax.rem(gather_col + flip, total)) & (gather_col < total)
    gram = jnp.dot(spread, gather.astype(jnp.float32), precision=HIGHEST, preferred_element_type=jnp.float32)

    def spread_sum(value, sender, receiver, mine, peers, peer_of, send_sems, recv_sems):
        sender[...] = value
        receiver[mine] = value
        for offset in range(1, peers):
            pltpu.make_async_remote_copy(
                src_ref=sender, dst_ref=receiver.at[mine],
                send_sem=send_sems.at[offset - 1], recv_sem=recv_sems.at[offset - 1],
                device_id=peer_of(offset), device_id_type=MESH).start()
        for offset in range(1, peers):
            origin = lax.rem(mine + peers - offset, peers)
            pltpu.make_async_remote_copy(
                src_ref=sender, dst_ref=receiver.at[origin],
                send_sem=send_sems.at[offset - 1], recv_sem=recv_sems.at[offset - 1],
                device_id=peer_of(offset), device_id_type=MESH).wait_recv()
        result = receiver[0]
        for n in range(1, peers):
            result = result + receiver[n]
        return result

    gram = spread_sum(gram, g_send, g_recv, place, team, team_peer, a_send, a_recv)
    gram = spread_sum(gram, s_send, s_recv, gz, n_gz, column_peer, b_send, b_recv)
    gram = gram * (1.0 / (planes * rows * width * n_gz * n_gy))

    line = lax.broadcasted_iota(jnp.int32, (total, 128), 0)
    column = lax.broadcasted_iota(jnp.int32, (total, 128), 1)
    system = gram + jnp.where(column == line + total, 1.0, 0.0)
    scaled = jnp.zeros_like(system)
    for c in range(total):
        row = jnp.broadcast_to(system[c:c + 1, :], (total, 128))
        factor = jnp.broadcast_to(system[:, c:c + 1], (total, 128))
        pivot = jnp.broadcast_to(factor[c:c + 1, :], (total, 128))
        scaled = jnp.where(line == c, system / jnp.sqrt(pivot), scaled)
        if c < total - 1:
            system = jnp.where(line > c, system - (factor / pivot) * row, system)
    fact[...] = jnp.where((column < line), 0.0, scaled)

    for phase in range(2):
        for direction in range(2):
            @pl.when(started(0, direction))
            def _():
                for group in range(groups):
                    z_copy(phase, direction, group).wait_send()

            @pl.when(started(1, direction))
            def _():
                y_copy(phase, direction).wait_send()
    bulk_copy.wait_send()
    for group in range(groups):
        for side in range(2):
            edge_copy(group, side).wait_send()
    for peers, sender, receiver, peer_of, send_sems, recv_sems in (
            (team, g_send, g_recv, team_peer, a_send, a_recv),
            (n_gz, s_send, s_recv, column_peer, b_send, b_recv)):
        for offset in range(1, peers):
            pltpu.make_async_remote_copy(
                src_ref=sender, dst_ref=receiver.at[0],
                send_sem=send_sems.at[offset - 1], recv_sem=recv_sems.at[offset - 1],
                device_id=peer_of(offset), device_id_type=MESH).wait_send()


def basis_kernel(scalars, fact, own, part, basis, triangle):
    count, _, rows, _ = own.shape
    total = 2 * count
    pa = lax.axis_index("pa")
    triangle[...] = fact[:, :total]
    first, other = pa * count, (1 - pa) * count

    z = pl.program_id(0)

    def step(i, carry):
        at = pl.ds(pl.multiple_of(i * 16, 16), 16)
        for k in range(count):
            value = scalars[first + k, total + first] * own[0, z, at, :]
            for j in range(1, k + 1):
                value = value + scalars[first + k, total + first + j] * own[j, z, at, :]
            basis[k, 0, at, :] = value

        @pl.when(pa > 0)
        def _():
            for k in range(count):
                value = basis[k, 0, at, :]
                for j in range(count):
                    value = value + scalars[first + k, total + other + j] * part[j, z, at, :]
                basis[k, 0, at, :] = value
        return carry

    lax.fori_loop(0, rows // 16, step, 0)


def shards(probes, weight, courant, upwind_flags):
    count, planes, rows, width = probes.shape
    sizes = tuple(lax.axis_size(axis) for axis in ("gz", "gy", "pa"))
    n_gz, n_gy, n_pa = sizes
    total = 2 * count
    team = n_gy * n_pa
    groups = count // GROUP
    f32 = jnp.float32
    dma = pltpu.SemaphoreType.DMA
    in_hbm = pl.BlockSpec(memory_space=pltpu.HBM)
    held = pl.BlockSpec(memory_space=pltpu.VMEM)
    y_own, y_part, fact = pl.pallas_call(
        functools.partial(sketch_kernel, sizes),
        out_shape=(
            pltpu.VMEM(probes.shape, f32),
            pltpu.VMEM(probes.shape, f32),
            pltpu.VMEM((total, 128), f32),
        ),
        in_specs=[in_hbm] * 4,
        out_specs=(held, held, held),
        scratch_shapes=[
            pltpu.VMEM((count, planes + 2, rows + 2 * PAD, width), f32),
            pltpu.VMEM((count, planes + 2, rows + 2 * PAD, width), f32),
            pltpu.VMEM(courant.shape, f32),
            pltpu.VMEM(upwind_flags.shape, jnp.int32),
            pltpu.VMEM(weight.shape, f32),
            pltpu.VMEM((2, planes, rows, width), f32),
            pltpu.VMEM((total * total, 8, 128), f32),
            pltpu.VMEM((total * total, 128), f32),
            pltpu.VMEM((total, 128), f32),
            pltpu.VMEM((team, total, 128), f32),
            pltpu.VMEM((total, 128), f32),
            pltpu.VMEM((n_gz, total, 128), f32),
            dma((4,)),
            dma((2, 2, groups)),
            dma((2, 2, groups)),
            dma((2, 2)),
            dma((2, 2)),
            dma((1 + 2 * groups,)),
            dma((1 + 2 * groups,)),
            dma((team,)),
            dma((team,)),
            dma((n_gz,)),
            dma((n_gz,)),
        ],
        compiler_params=pltpu.CompilerParams(
            collective_id=0, has_side_effects=True, vmem_limit_bytes=54 * 1024 * 1024),
        name="sketch",
    )(probes, weight, courant, upwind_flags)
    block = pl.BlockSpec((count, 1, rows, width), lambda z: (0, z, 0, 0))
    return pl.pallas_call(
        basis_kernel,
        grid=(planes,),
        out_shape=(
            jax.ShapeDtypeStruct(probes.shape, f32),
            jax.ShapeDtypeStruct((total, total), f32),
        ),
        in_specs=[
            pl.BlockSpec(memory_space=pltpu.SMEM),
            pl.BlockSpec((total, 128), lambda z: (0, 0)),
            held,
            held,
        ],
        out_specs=(block, pl.BlockSpec((total, total), lambda z: (0, 0))),
        compiler_params=pltpu.CompilerParams(vmem_limit_bytes=16 * 1024 * 1024),
        name="basis",
    )(fact, fact, y_own, y_part)


def solution(mesh):
    placed = (
        P("pa", "gz", "gy", None),
        P("gz", "gy", None),
        P(None, None, "gz", "gy", None),
        P(None, None, "gz", "gy", None),
    )
    return jax.shard_map(
        shards,
        mesh=mesh,
        in_specs=placed,
        out_specs=(P("pa", "gz", "gy", None), P()),
        check_vma=False,
    )
```

```python
import functools

import jax
import jax.numpy as jnp
from jax import lax
from jax.experimental import pallas as pl
from jax.experimental.pallas import tpu as pltpu
from jax.sharding import PartitionSpec as P

MESH = pl.DeviceIdType.MESH
HIGHEST = lax.Precision.HIGHEST
GROUP = 2
PAD = 8


def sketch_kernel(sizes, probes, weight, courant, flags, own, part, fact,
                  u0, u1, cbuf, fbuf, wbuf, centre, gacc, pairs, g_send, g_recv, s_send, s_recv,
                  load_sems, zs_send, zs_recv, ys_send, ys_recv, ps_send, ps_recv,
                  a_send, a_recv, b_send, b_recv,
                  r_send, r_recv, pl_send, pl_recv):
    n_gz, n_gy, n_pa = sizes
    count, planes, rows, width = probes.shape
    groups = count // GROUP
    tiles = rows // 8
    gz, gy, pa = lax.axis_index("gz"), lax.axis_index("gy"), lax.axis_index("pa")
    body = pl.ds(PAD, rows)
    inner = pl.ds(1, planes)

    loads = [
        pltpu.make_async_copy(probes, u0.at[:, inner, body, :], load_sems.at[0]),
        pltpu.make_async_copy(courant, cbuf, load_sems.at[1]),
        pltpu.make_async_copy(flags, fbuf, load_sems.at[2]),
        pltpu.make_async_copy(weight, wbuf, load_sems.at[3]),
    ]
    for load in loads:
        load.start()

    team = n_gy * n_pa
    place = gy * n_pa + pa

    def team_peer(offset):
        other = lax.rem(place + offset, team)
        return {"gy": other // n_pa, "pa": lax.rem(other, n_pa)}

    def column_peer(offset):
        return {"gz": lax.rem(gz + offset, n_gz)}

    barrier = pltpu.get_barrier_semaphore()
    for offset in range(1, team):
        pl.semaphore_signal(barrier, inc=1, device_id=team_peer(offset), device_id_type=MESH)
    for offset in range(1, n_gz):
        pl.semaphore_signal(barrier, inc=1, device_id=column_peer(offset), device_id_type=MESH)
    pl.semaphore_wait(barrier, team + n_gz - 2)

    has_next = (gz < n_gz - 1, gy < n_gy - 1)
    has_before = (gz > 0, gy > 0)

    def z_copy(phase, direction, group):
        picked = pl.ds(group * GROUP, GROUP)
        source_plane = planes - 1 if direction == 0 else 0
        target_plane = 0 if direction == 0 else planes + 1
        if phase == 0:
            source = probes.at[picked, source_plane]
        else:
            source = u1.at[picked, source_plane + 1, body, :]
        target = (u0, u1)[phase].at[picked, target_plane, body, :]
        step = 1 if direction == 0 else n_gz - 1
        return pltpu.make_async_remote_copy(
            src_ref=source, dst_ref=target,
            send_sem=zs_send.at[phase, direction, group], recv_sem=zs_recv.at[phase, direction, group],
            device_id={"gz": lax.rem(gz + step, n_gz)}, device_id_type=MESH)

    def y_copy(phase, direction):
        source_row = rows - 1 if direction == 0 else 0
        target_row = PAD - 1 if direction == 0 else PAD + rows
        if phase == 0:
            source = probes.at[:, :, pl.ds(source_row, 1), :]
        else:
            source = u1.at[:, inner, pl.ds(source_row + PAD, 1), :]
        target = (u0, u1)[phase].at[:, inner, pl.ds(target_row, 1), :]
        step = 1 if direction == 0 else n_gy - 1
        return pltpu.make_async_remote_copy(
            src_ref=source, dst_ref=target,
            send_sem=ys_send.at[phase, direction], recv_sem=ys_recv.at[phase, direction],
            device_id={"gy": lax.rem(gy + step, n_gy)}, device_id_type=MESH)

    def started(axis, direction):
        return has_next[axis] if direction == 0 else has_before[axis]

    def awaited(axis, direction):
        return has_before[axis] if direction == 0 else has_next[axis]

    def start_z(phase, group):
        for direction in range(2):
            @pl.when(started(0, direction))
            def _():
                z_copy(phase, direction, group).start()

    def wait_z(phase, group):
        for direction in range(2):
            @pl.when(awaited(0, direction))
            def _():
                z_copy(phase, direction, group).wait_recv()

    def start_y(phase):
        for direction in range(2):
            @pl.when(started(1, direction))
            def _():
                y_copy(phase, direction).start()

    def wait_y(phase):
        for direction in range(2):
            @pl.when(awaited(1, direction))
            def _():
                y_copy(phase, direction).wait_recv()

    start_y(0)
    for group in range(groups):
        start_z(0, group)

    for buffer in (u0, u1):
        for direction in range(2):
            plane = 0 if direction == 0 else planes + 1
            row = PAD - 1 if direction == 0 else PAD + rows

            @pl.when(jnp.logical_not(awaited(0, direction)))
            def _():
                def clear(k, carry):
                    buffer[k, plane, PAD:PAD + rows, :] = jnp.zeros((rows, width), jnp.float32)
                    return carry
                lax.fori_loop(0, count, clear, 0)

            @pl.when(jnp.logical_not(awaited(1, direction)))
            def _():
                def clear(i, carry):
                    buffer[i // planes, 1 + lax.rem(i, planes), row:row + 1, :] = jnp.zeros((1, width), jnp.float32)
                    return carry
                lax.fori_loop(0, count * planes, clear, 0)

    loads[1].wait()
    loads[2].wait()
    lane = lax.broadcasted_iota(jnp.int32, (rows, width), 1)

    def prepare(i, carry):
        s, z = i // planes, lax.rem(i, planes)
        cx = cbuf[s, 2, z]
        centre[s, z] = 1.0 - (cbuf[s, 0, z] + cbuf[s, 1, z] + cx)
        edge = jnp.where(fbuf[s, 2, z] == 1, 0, width - 1)
        cbuf[s, 2, z] = jnp.where(lane == edge, 0.0, cx)
        return carry

    lax.fori_loop(0, 2 * planes, prepare, 0)

    def advance(source, s, z, first, store):
        for tile in range(tiles):
            low = tile * 8
            here = (slice(low, low + 8), slice(None))
            c0 = centre[(s, z) + here]
            cz, cy, cx = (cbuf[(s, d, z) + here] for d in range(3))
            fz, fy, fx = (fbuf[(s, d, z) + here] == 1 for d in range(3))
            at = PAD + low
            for k in range(GROUP):
                number = first + k
                u = source[number, z + 1, at:at + 8, :]
                n_z = jnp.where(fz, source[number, z, at:at + 8, :], source[number, z + 2, at:at + 8, :])
                n_y = jnp.where(fy, source[number, z + 1, at - 1:at + 7, :], source[number, z + 1, at + 1:at + 9, :])
                n_x = jnp.where(fx, pltpu.roll(u, 1, 1), pltpu.roll(u, width - 1, 1))
                store(number, z, low, c0 * u + cz * n_z + cy * n_y + cx * n_x)

    def store_first(number, z, low, value):
        u1[number, z + 1, PAD + low:PAD + low + 8, :] = value

    def store_sketch(number, z, low, value):
        own[number, z, low:low + 8, :] = wbuf[z, low:low + 8, :] * value

    def sweep_inner(source, s, store, before, after):
        def plane(i, carry):
            before(1 + i)

            def step(group, carry):
                advance(source, s, 1 + i, group * GROUP, store)
                return carry
            lax.fori_loop(0, groups, step, 0)
            after(1 + i)
            return carry
        lax.fori_loop(0, planes - 2, plane, 0)

    def row_copy(direction, z):
        source_row = PAD + rows - 1 if direction == 0 else PAD
        target_row = PAD - 1 if direction == 0 else PAD + rows
        step = 1 if direction == 0 else n_gy - 1
        return pltpu.make_async_remote_copy(
            src_ref=u1.at[:, z + 1, pl.ds(source_row, 1), :], dst_ref=u1.at[:, z + 1, pl.ds(target_row, 1), :],
            send_sem=r_send.at[direction, z], recv_sem=r_recv.at[direction, z],
            device_id={"gy": lax.rem(gy + step, n_gy)}, device_id_type=MESH)

    def start_rows(z):
        for direction in range(2):
            @pl.when(started(1, direction))
            def _():
                row_copy(direction, z).start()

    def wait_rows(z):
        for direction in range(2):
            @pl.when(awaited(1, direction))
            def _():
                row_copy(direction, z).wait_recv()

    def plane_copy(z):
        return pltpu.make_async_remote_copy(
            src_ref=own.at[:, z], dst_ref=part.at[:, z],
            send_sem=pl_send.at[z], recv_sem=pl_recv.at[z],
            device_id={"pa": lax.rem(pa + 1, n_pa)}, device_id_type=MESH)

    def start_plane(z):
        plane_copy(z).start()

    def nothing(z):
        pass

    def sweep_edges(source, s, group, store):
        def step(i, carry):
            advance(source, s, i * (planes - 1), group * GROUP, store)
            return carry
        lax.fori_loop(0, 2, step, 0)

    loads[0].wait()
    loads[3].wait()
    wait_y(0)
    sweep_inner(u0, 0, store_first, nothing, start_rows)
    for group in range(groups):
        wait_z(0, group)
        sweep_edges(u0, 0, group, store_first)
        start_z(1, group)
    for z in (0, planes - 1):
        start_rows(z)
    sweep_inner(u1, 1, store_sketch, wait_rows, start_plane)

    def edge_copy(group, side):
        picked = (pl.ds(group * GROUP, GROUP), side * (planes - 1))
        index = 1 + 2 * group + side
        return pltpu.make_async_remote_copy(
            src_ref=own.at[picked], dst_ref=part.at[picked],
            send_sem=ps_send.at[index], recv_sem=ps_recv.at[index],
            device_id={"pa": lax.rem(pa + 1, n_pa)}, device_id_type=MESH)

    total = 2 * count
    half = count // 2
    blocks = [
        [(a, b) for a in range(count) for b in range(a, count)],
        [(a, b) for a in range(count, total) for b in range(a, total)],
        [(a, b) for a in range(half) for b in range(count, total)],
        [(a, b) for a in range(half, count) for b in range(count, total)],
    ]

    def products(first_plane, plane_count, begin):
        for block in blocks:
            used = sorted({i for pair in block for i in pair})

            def step(i, sums, block=block, used=used):
                z = first_plane + i // tiles
                at = pl.ds(pl.multiple_of(lax.rem(i, tiles) * 8, 8), 8)
                sums = list(sums)
                for piece in range(width // 128):
                    cells = slice(piece * 128, piece * 128 + 128)
                    rows_now = {}
                    for n in used:
                        holder = own if n < count else part
                        rows_now[n] = holder[n % count, z, at, cells]
                    for spot, (a, b) in enumerate(block):
                        sums[spot] = sums[spot] + rows_now[a] * rows_now[b]
                return tuple(sums)

            if begin:
                sums = tuple(jnp.zeros((8, 128), jnp.float32) for _ in block)
            else:
                sums = tuple(gacc[a * total + b] for a, b in block)
            sums = lax.fori_loop(0, plane_count * tiles, step, sums)
            for (a, b), value in zip(block, sums):
                if begin:
                    gacc[a * total + b] = value
                else:
                    line = jnp.sum(value, axis=0, keepdims=True)
                    pairs[a * total + b:a * total + b + 1, :] = line
                    if a != b:
                        pairs[b * total + a:b * total + a + 1, :] = line

    for z in range(1, planes - 1):
        plane_copy(z).wait_recv()
    quarter = planes // 2 - 1
    products(1 + quarter * pa, quarter, True)

    for z in (0, planes - 1):
        wait_rows(z)
    for group in range(groups):
        wait_z(1, group)
        sweep_edges(u1, 1, group, store_sketch)
        for side in range(2):
            edge_copy(group, side).start()
    for group in range(groups):
        for side in range(2):
            edge_copy(group, side).wait_recv()
    products((planes - 1) * pa, 1, False)

    flip = pa * count
    entries = total * total
    summed = lax.dot_general(jnp.ones((8, 128), jnp.float32), pairs[...], (((1,), (1,)), ((), ())),
                             precision=HIGHEST, preferred_element_type=jnp.float32)
    spread_row = lax.broadcasted_iota(jnp.int32, (total, entries), 0)
    spread_col = lax.broadcasted_iota(jnp.int32, (total, entries), 1)
    picked_row = lax.rem(spread_row + flip, total) == spread_col // total
    spread = jnp.where(picked_row, jnp.broadcast_to(summed[0:1, :], (total, entries)), 0.0)
    gather_row = lax.broadcasted_iota(jnp.int32, (entries, 128), 0)
    gather_col = lax.broadcasted_iota(jnp.int32, (entries, 128), 1)
    gather = (lax.rem(gather_row, total) == lax.rem(gather_col + flip, total)) & (gather_col < total)
    gram = jnp.dot(spread, gather.astype(jnp.float32), precision=HIGHEST, preferred_element_type=jnp.float32)

    def spread_sum(value, sender, receiver, mine, peers, peer_of, send_sems, recv_sems):
        sender[...] = value
        receiver[mine] = value
        for offset in range(1, peers):
            pltpu.make_async_remote_copy(
                src_ref=sender, dst_ref=receiver.at[mine],
                send_sem=send_sems.at[offset - 1], recv_sem=recv_sems.at[offset - 1],
                device_id=peer_of(offset), device_id_type=MESH).start()
        for offset in range(1, peers):
            origin = lax.rem(mine + peers - offset, peers)
            pltpu.make_async_remote_copy(
                src_ref=sender, dst_ref=receiver.at[origin],
                send_sem=send_sems.at[offset - 1], recv_sem=recv_sems.at[offset - 1],
                device_id=peer_of(offset), device_id_type=MESH).wait_recv()
        result = receiver[0]
        for n in range(1, peers):
            result = result + receiver[n]
        return result

    gram = spread_sum(gram, g_send, g_recv, place, team, team_peer, a_send, a_recv)
    gram = spread_sum(gram, s_send, s_recv, gz, n_gz, column_peer, b_send, b_recv)
    gram = gram * (1.0 / (planes * rows * width * n_gz * n_gy))

    line = lax.broadcasted_iota(jnp.int32, (total, 128), 0)
    column = lax.broadcasted_iota(jnp.int32, (total, 128), 1)
    system = gram + jnp.where(column == line + total, 1.0, 0.0)
    scaled = jnp.zeros_like(system)
    for c in range(total):
        row = jnp.broadcast_to(system[c:c + 1, :], (total, 128))
        factor = jnp.broadcast_to(system[:, c:c + 1], (total, 128))
        pivot = jnp.broadcast_to(factor[c:c + 1, :], (total, 128))
        scaled = jnp.where(line == c, system / jnp.sqrt(pivot), scaled)
        if c < total - 1:
            system = jnp.where(line > c, system - (factor / pivot) * row, system)
    fact[...] = jnp.where((column < line), 0.0, scaled)

    for phase in range(2):
        for direction in range(2):
            @pl.when(started(0, direction))
            def _():
                for group in range(groups):
                    z_copy(phase, direction, group).wait_send()

    for direction in range(2):
        @pl.when(started(1, direction))
        def _():
            y_copy(0, direction).wait_send()
            for z in range(planes):
                row_copy(direction, z).wait_send()
    for z in range(1, planes - 1):
        plane_copy(z).wait_send()
    for group in range(groups):
        for side in range(2):
            edge_copy(group, side).wait_send()
    for peers, sender, receiver, peer_of, send_sems, recv_sems in (
            (team, g_send, g_recv, team_peer, a_send, a_recv),
            (n_gz, s_send, s_recv, column_peer, b_send, b_recv)):
        for offset in range(1, peers):
            pltpu.make_async_remote_copy(
                src_ref=sender, dst_ref=receiver.at[0],
                send_sem=send_sems.at[offset - 1], recv_sem=recv_sems.at[offset - 1],
                device_id=peer_of(offset), device_id_type=MESH).wait_send()


def basis_kernel(scalars, fact, own, part, basis, triangle):
    count, _, rows, _ = own.shape
    total = 2 * count
    pa = lax.axis_index("pa")
    triangle[...] = fact[:, :total]
    first, other = pa * count, (1 - pa) * count

    z = pl.program_id(0)

    def step(i, carry):
        at = pl.ds(pl.multiple_of(i * 16, 16), 16)
        for k in range(count):
            value = scalars[first + k, total + first] * own[0, z, at, :]
            for j in range(1, k + 1):
                value = value + scalars[first + k, total + first + j] * own[j, z, at, :]
            basis[k, 0, at, :] = value

        @pl.when(pa > 0)
        def _():
            for k in range(count):
                value = basis[k, 0, at, :]
                for j in range(count):
                    value = value + scalars[first + k, total + other + j] * part[j, z, at, :]
                basis[k, 0, at, :] = value
        return carry

    lax.fori_loop(0, rows // 16, step, 0)


def shards(probes, weight, courant, upwind_flags):
    count, planes, rows, width = probes.shape
    sizes = tuple(lax.axis_size(axis) for axis in ("gz", "gy", "pa"))
    n_gz, n_gy, n_pa = sizes
    total = 2 * count
    team = n_gy * n_pa
    groups = count // GROUP
    f32 = jnp.float32
    dma = pltpu.SemaphoreType.DMA
    in_hbm = pl.BlockSpec(memory_space=pltpu.HBM)
    held = pl.BlockSpec(memory_space=pltpu.VMEM)
    y_own, y_part, fact = pl.pallas_call(
        functools.partial(sketch_kernel, sizes),
        out_shape=(
            pltpu.VMEM(probes.shape, f32),
            pltpu.VMEM(probes.shape, f32),
            pltpu.VMEM((total, 128), f32),
        ),
        in_specs=[in_hbm] * 4,
        out_specs=(held, held, held),
        scratch_shapes=[
            pltpu.VMEM((count, planes + 2, rows + 2 * PAD, width), f32),
            pltpu.VMEM((count, planes + 2, rows + 2 * PAD, width), f32),
            pltpu.VMEM(courant.shape, f32),
            pltpu.VMEM(upwind_flags.shape, jnp.int32),
            pltpu.VMEM(weight.shape, f32),
            pltpu.VMEM((2, planes, rows, width), f32),
            pltpu.VMEM((total * total, 8, 128), f32),
            pltpu.VMEM((total * total, 128), f32),
            pltpu.VMEM((total, 128), f32),
            pltpu.VMEM((team, total, 128), f32),
            pltpu.VMEM((total, 128), f32),
            pltpu.VMEM((n_gz, total, 128), f32),
            dma((4,)),
            dma((2, 2, groups)),
            dma((2, 2, groups)),
            dma((2, 2)),
            dma((2, 2)),
            dma((1 + 2 * groups,)),
            dma((1 + 2 * groups,)),
            dma((team,)),
            dma((team,)),
            dma((n_gz,)),
            dma((n_gz,)),
            dma((2, planes)),
            dma((2, planes)),
            dma((planes,)),
            dma((planes,)),
        ],
        compiler_params=pltpu.CompilerParams(
            collective_id=0, has_side_effects=True, vmem_limit_bytes=54 * 1024 * 1024),
        name="sketch",
    )(probes, weight, courant, upwind_flags)
    block = pl.BlockSpec((count, 1, rows, width), lambda z: (0, z, 0, 0))
    return pl.pallas_call(
        basis_kernel,
        grid=(planes,),
        out_shape=(
            jax.ShapeDtypeStruct(probes.shape, f32),
            jax.ShapeDtypeStruct((total, total), f32),
        ),
        in_specs=[
            pl.BlockSpec(memory_space=pltpu.SMEM),
            pl.BlockSpec((total, 128), lambda z: (0, 0)),
            held,
            held,
        ],
        out_specs=(block, pl.BlockSpec((total, total), lambda z: (0, 0))),
        compiler_params=pltpu.CompilerParams(vmem_limit_bytes=16 * 1024 * 1024),
        name="basis",
    )(fact, fact, y_own, y_part)


def solution(mesh):
    placed = (
        P("pa", "gz", "gy", None),
        P("gz", "gy", None),
        P(None, None, "gz", "gy", None),
        P(None, None, "gz", "gy", None),
    )
    return jax.shard_map(
        shards,
        mesh=mesh,
        in_specs=placed,
        out_specs=(P("pa", "gz", "gy", None), P()),
        check_vma=False,
    )
```

```python
import functools

import jax
import jax.numpy as jnp
from jax import lax
from jax.experimental import pallas as pl
from jax.experimental.pallas import tpu as pltpu
from jax.sharding import PartitionSpec as P

MESH = pl.DeviceIdType.MESH
HIGHEST = lax.Precision.HIGHEST
GROUP = 2
PAD = 8


def sketch_kernel(sizes, probes, weight, courant, flags, own, part, fact,
                  u0, u1, cbuf, fbuf, wbuf, centre, gacc, pairs, g_send, g_recv, s_send, s_recv,
                  load_sems, zs_send, zs_recv, ys_send, ys_recv, ps_send, ps_recv,
                  a_send, a_recv, b_send, b_recv,
                  r_send, r_recv, pl_send, pl_recv):
    n_gz, n_gy, n_pa = sizes
    count, planes, rows, width = probes.shape
    groups = count // GROUP
    tiles = rows // 8
    gz, gy, pa = lax.axis_index("gz"), lax.axis_index("gy"), lax.axis_index("pa")
    body = pl.ds(PAD, rows)
    inner = pl.ds(1, planes)

    loads = [
        pltpu.make_async_copy(probes, u0.at[:, inner, body, :], load_sems.at[0]),
        pltpu.make_async_copy(courant, cbuf, load_sems.at[1]),
        pltpu.make_async_copy(flags, fbuf, load_sems.at[2]),
        pltpu.make_async_copy(weight, wbuf, load_sems.at[3]),
    ]
    for load in loads:
        load.start()

    team = n_gy * n_pa
    place = gy * n_pa + pa

    def team_peer(offset):
        other = lax.rem(place + offset, team)
        return {"gy": other // n_pa, "pa": lax.rem(other, n_pa)}

    def column_peer(offset):
        return {"gz": lax.rem(gz + offset, n_gz)}

    barrier = pltpu.get_barrier_semaphore()
    for offset in range(1, team):
        pl.semaphore_signal(barrier, inc=1, device_id=team_peer(offset), device_id_type=MESH)
    for offset in range(1, n_gz):
        pl.semaphore_signal(barrier, inc=1, device_id=column_peer(offset), device_id_type=MESH)
    pl.semaphore_wait(barrier, team + n_gz - 2)

    has_next = (gz < n_gz - 1, gy < n_gy - 1)
    has_before = (gz > 0, gy > 0)

    def z_copy(phase, direction, group):
        picked = pl.ds(group * GROUP, GROUP)
        source_plane = planes - 1 if direction == 0 else 0
        target_plane = 0 if direction == 0 else planes + 1
        if phase == 0:
            source = probes.at[picked, source_plane]
        else:
            source = u1.at[picked, source_plane + 1, body, :]
        target = (u0, u1)[phase].at[picked, target_plane, body, :]
        step = 1 if direction == 0 else n_gz - 1
        return pltpu.make_async_remote_copy(
            src_ref=source, dst_ref=target,
            send_sem=zs_send.at[phase, direction, group], recv_sem=zs_recv.at[phase, direction, group],
            device_id={"gz": lax.rem(gz + step, n_gz)}, device_id_type=MESH)

    def first_rows(direction, z):
        source_row = rows - 1 if direction == 0 else 0
        target_row = PAD - 1 if direction == 0 else PAD + rows
        step = 1 if direction == 0 else n_gy - 1
        return pltpu.make_async_remote_copy(
            src_ref=probes.at[:, z, pl.ds(source_row, 1), :], dst_ref=u0.at[:, z + 1, pl.ds(target_row, 1), :],
            send_sem=ys_send.at[direction, z], recv_sem=ys_recv.at[direction, z],
            device_id={"gy": lax.rem(gy + step, n_gy)}, device_id_type=MESH)

    def started(axis, direction):
        return has_next[axis] if direction == 0 else has_before[axis]

    def awaited(axis, direction):
        return has_before[axis] if direction == 0 else has_next[axis]

    def start_z(phase, group):
        for direction in range(2):
            @pl.when(started(0, direction))
            def _():
                z_copy(phase, direction, group).start()

    def wait_z(phase, group):
        for direction in range(2):
            @pl.when(awaited(0, direction))
            def _():
                z_copy(phase, direction, group).wait_recv()

    def wait_first(z):
        for direction in range(2):
            @pl.when(awaited(1, direction))
            def _():
                first_rows(direction, z).wait_recv()

    for z in [*range(1, planes - 1), 0, planes - 1]:
        for direction in range(2):
            @pl.when(started(1, direction))
            def _():
                first_rows(direction, z).start()
    for group in range(groups):
        start_z(0, group)

    for buffer in (u0, u1):
        for direction in range(2):
            plane = 0 if direction == 0 else planes + 1
            row = PAD - 1 if direction == 0 else PAD + rows

            @pl.when(jnp.logical_not(awaited(0, direction)))
            def _():
                def clear(k, carry):
                    buffer[k, plane, PAD:PAD + rows, :] = jnp.zeros((rows, width), jnp.float32)
                    return carry
                lax.fori_loop(0, count, clear, 0)

            @pl.when(jnp.logical_not(awaited(1, direction)))
            def _():
                def clear(i, carry):
                    buffer[i // planes, 1 + lax.rem(i, planes), row:row + 1, :] = jnp.zeros((1, width), jnp.float32)
                    return carry
                lax.fori_loop(0, count * planes, clear, 0)

    loads[1].wait()
    loads[2].wait()
    lane = lax.broadcasted_iota(jnp.int32, (rows, width), 1)

    def prepare(i, carry):
        s, z = i // planes, lax.rem(i, planes)
        cx = cbuf[s, 2, z]
        centre[s, z] = 1.0 - (cbuf[s, 0, z] + cbuf[s, 1, z] + cx)
        edge = jnp.where(fbuf[s, 2, z] == 1, 0, width - 1)
        cbuf[s, 2, z] = jnp.where(lane == edge, 0.0, cx)
        return carry

    lax.fori_loop(0, 2 * planes, prepare, 0)

    def advance(source, s, z, first, store):
        for tile in range(tiles):
            low = tile * 8
            here = (slice(low, low + 8), slice(None))
            c0 = centre[(s, z) + here]
            cz, cy, cx = (cbuf[(s, d, z) + here] for d in range(3))
            fz, fy, fx = (fbuf[(s, d, z) + here] == 1 for d in range(3))
            at = PAD + low
            for k in range(GROUP):
                number = first + k
                u = source[number, z + 1, at:at + 8, :]
                n_z = jnp.where(fz, source[number, z, at:at + 8, :], source[number, z + 2, at:at + 8, :])
                n_y = jnp.where(fy, source[number, z + 1, at - 1:at + 7, :], source[number, z + 1, at + 1:at + 9, :])
                n_x = jnp.where(fx, pltpu.roll(u, 1, 1), pltpu.roll(u, width - 1, 1))
                store(number, z, low, c0 * u + cz * n_z + cy * n_y + cx * n_x)

    def store_first(number, z, low, value):
        u1[number, z + 1, PAD + low:PAD + low + 8, :] = value

    def store_sketch(number, z, low, value):
        own[number, z, low:low + 8, :] = wbuf[z, low:low + 8, :] * value

    def sweep_inner(source, s, store, before, after):
        def plane(i, carry):
            before(1 + i)

            def step(group, carry):
                advance(source, s, 1 + i, group * GROUP, store)
                return carry
            lax.fori_loop(0, groups, step, 0)
            after(1 + i)
            return carry
        lax.fori_loop(0, planes - 2, plane, 0)

    def row_copy(direction, z):
        source_row = PAD + rows - 1 if direction == 0 else PAD
        target_row = PAD - 1 if direction == 0 else PAD + rows
        step = 1 if direction == 0 else n_gy - 1
        return pltpu.make_async_remote_copy(
            src_ref=u1.at[:, z + 1, pl.ds(source_row, 1), :], dst_ref=u1.at[:, z + 1, pl.ds(target_row, 1), :],
            send_sem=r_send.at[direction, z], recv_sem=r_recv.at[direction, z],
            device_id={"gy": lax.rem(gy + step, n_gy)}, device_id_type=MESH)

    def start_rows(z):
        for direction in range(2):
            @pl.when(started(1, direction))
            def _():
                row_copy(direction, z).start()

    def wait_rows(z):
        for direction in range(2):
            @pl.when(awaited(1, direction))
            def _():
                row_copy(direction, z).wait_recv()

    def plane_copy(z):
        return pltpu.make_async_remote_copy(
            src_ref=own.at[:, z], dst_ref=part.at[:, z],
            send_sem=pl_send.at[z], recv_sem=pl_recv.at[z],
            device_id={"pa": lax.rem(pa + 1, n_pa)}, device_id_type=MESH)

    def start_plane(z):
        plane_copy(z).start()

    def sweep_edges(source, s, group, store):
        def step(i, carry):
            advance(source, s, i * (planes - 1), group * GROUP, store)
            return carry
        lax.fori_loop(0, 2, step, 0)

    loads[0].wait()
    loads[3].wait()
    sweep_inner(u0, 0, store_first, wait_first, start_rows)
    for z in (0, planes - 1):
        wait_first(z)
    for group in range(groups):
        wait_z(0, group)
        sweep_edges(u0, 0, group, store_first)
        start_z(1, group)
    for z in (0, planes - 1):
        start_rows(z)
    sweep_inner(u1, 1, store_sketch, wait_rows, start_plane)

    def edge_copy(group, side):
        picked = (pl.ds(group * GROUP, GROUP), side * (planes - 1))
        index = 1 + 2 * group + side
        return pltpu.make_async_remote_copy(
            src_ref=own.at[picked], dst_ref=part.at[picked],
            send_sem=ps_send.at[index], recv_sem=ps_recv.at[index],
            device_id={"pa": lax.rem(pa + 1, n_pa)}, device_id_type=MESH)

    total = 2 * count
    half = count // 2
    blocks = [
        [(a, b) for a in range(count) for b in range(a, count)],
        [(a, b) for a in range(count, total) for b in range(a, total)],
        [(a, b) for a in range(half) for b in range(count, total)],
        [(a, b) for a in range(half, count) for b in range(count, total)],
    ]

    def products(first_plane, plane_count, begin):
        for block in blocks:
            used = sorted({i for pair in block for i in pair})

            def step(i, sums, block=block, used=used):
                z = first_plane + i // tiles
                at = pl.ds(pl.multiple_of(lax.rem(i, tiles) * 8, 8), 8)
                sums = list(sums)
                for piece in range(width // 128):
                    cells = slice(piece * 128, piece * 128 + 128)
                    rows_now = {}
                    for n in used:
                        holder = own if n < count else part
                        rows_now[n] = holder[n % count, z, at, cells]
                    for spot, (a, b) in enumerate(block):
                        sums[spot] = sums[spot] + rows_now[a] * rows_now[b]
                return tuple(sums)

            if begin:
                sums = tuple(jnp.zeros((8, 128), jnp.float32) for _ in block)
            else:
                sums = tuple(gacc[a * total + b] for a, b in block)
            sums = lax.fori_loop(0, plane_count * tiles, step, sums)
            for (a, b), value in zip(block, sums):
                if begin:
                    gacc[a * total + b] = value
                else:
                    line = jnp.sum(value, axis=0, keepdims=True)
                    pairs[a * total + b:a * total + b + 1, :] = line
                    if a != b:
                        pairs[b * total + a:b * total + a + 1, :] = line

    for z in range(1, planes - 1):
        plane_copy(z).wait_recv()
    quarter = planes // 2 - 1
    products(1 + quarter * pa, quarter, True)

    for z in (0, planes - 1):
        wait_rows(z)
    for group in range(groups):
        wait_z(1, group)
        sweep_edges(u1, 1, group, store_sketch)
        for side in range(2):
            edge_copy(group, side).start()
    for group in range(groups):
        for side in range(2):
            edge_copy(group, side).wait_recv()
    products((planes - 1) * pa, 1, False)

    flip = pa * count
    entries = total * total
    summed = lax.dot_general(jnp.ones((8, 128), jnp.float32), pairs[...], (((1,), (1,)), ((), ())),
                             precision=HIGHEST, preferred_element_type=jnp.float32)
    spread_row = lax.broadcasted_iota(jnp.int32, (total, entries), 0)
    spread_col = lax.broadcasted_iota(jnp.int32, (total, entries), 1)
    picked_row = lax.rem(spread_row + flip, total) == spread_col // total
    spread = jnp.where(picked_row, jnp.broadcast_to(summed[0:1, :], (total, entries)), 0.0)
    gather_row = lax.broadcasted_iota(jnp.int32, (entries, 128), 0)
    gather_col = lax.broadcasted_iota(jnp.int32, (entries, 128), 1)
    gather = (lax.rem(gather_row, total) == lax.rem(gather_col + flip, total)) & (gather_col < total)
    gram = jnp.dot(spread, gather.astype(jnp.float32), precision=HIGHEST, preferred_element_type=jnp.float32)

    def spread_sum(value, sender, receiver, mine, peers, peer_of, send_sems, recv_sems):
        sender[...] = value
        receiver[mine] = value
        for offset in range(1, peers):
            pltpu.make_async_remote_copy(
                src_ref=sender, dst_ref=receiver.at[mine],
                send_sem=send_sems.at[offset - 1], recv_sem=recv_sems.at[offset - 1],
                device_id=peer_of(offset), device_id_type=MESH).start()
        for offset in range(1, peers):
            origin = lax.rem(mine + peers - offset, peers)
            pltpu.make_async_remote_copy(
                src_ref=sender, dst_ref=receiver.at[origin],
                send_sem=send_sems.at[offset - 1], recv_sem=recv_sems.at[offset - 1],
                device_id=peer_of(offset), device_id_type=MESH).wait_recv()
        result = receiver[0]
        for n in range(1, peers):
            result = result + receiver[n]
        return result

    gram = spread_sum(gram, g_send, g_recv, place, team, team_peer, a_send, a_recv)
    gram = spread_sum(gram, s_send, s_recv, gz, n_gz, column_peer, b_send, b_recv)
    gram = gram * (1.0 / (planes * rows * width * n_gz * n_gy))

    line = lax.broadcasted_iota(jnp.int32, (total, 128), 0)
    column = lax.broadcasted_iota(jnp.int32, (total, 128), 1)
    system = gram + jnp.where(column == line + total, 1.0, 0.0)
    scaled = jnp.zeros_like(system)
    for c in range(total):
        row = jnp.broadcast_to(system[c:c + 1, :], (total, 128))
        factor = jnp.broadcast_to(system[:, c:c + 1], (total, 128))
        pivot = jnp.broadcast_to(factor[c:c + 1, :], (total, 128))
        scaled = jnp.where(line == c, system / jnp.sqrt(pivot), scaled)
        if c < total - 1:
            system = jnp.where(line > c, system - (factor / pivot) * row, system)
    fact[...] = jnp.where((column < line), 0.0, scaled)

    for phase in range(2):
        for direction in range(2):
            @pl.when(started(0, direction))
            def _():
                for group in range(groups):
                    z_copy(phase, direction, group).wait_send()

    for direction in range(2):
        @pl.when(started(1, direction))
        def _():
            for z in range(planes):
                first_rows(direction, z).wait_send()
                row_copy(direction, z).wait_send()
    for z in range(1, planes - 1):
        plane_copy(z).wait_send()
    for group in range(groups):
        for side in range(2):
            edge_copy(group, side).wait_send()
    for peers, sender, receiver, peer_of, send_sems, recv_sems in (
            (team, g_send, g_recv, team_peer, a_send, a_recv),
            (n_gz, s_send, s_recv, column_peer, b_send, b_recv)):
        for offset in range(1, peers):
            pltpu.make_async_remote_copy(
                src_ref=sender, dst_ref=receiver.at[0],
                send_sem=send_sems.at[offset - 1], recv_sem=recv_sems.at[offset - 1],
                device_id=peer_of(offset), device_id_type=MESH).wait_send()


def basis_kernel(scalars, fact, own, part, basis, triangle):
    count, _, rows, _ = own.shape
    total = 2 * count
    pa = lax.axis_index("pa")
    triangle[...] = fact[:, :total]
    first, other = pa * count, (1 - pa) * count

    z = pl.program_id(0)

    def step(i, carry):
        at = pl.ds(pl.multiple_of(i * 16, 16), 16)
        for k in range(count):
            value = scalars[first + k, total + first] * own[0, z, at, :]
            for j in range(1, k + 1):
                value = value + scalars[first + k, total + first + j] * own[j, z, at, :]
            basis[k, 0, at, :] = value

        @pl.when(pa > 0)
        def _():
            for k in range(count):
                value = basis[k, 0, at, :]
                for j in range(count):
                    value = value + scalars[first + k, total + other + j] * part[j, z, at, :]
                basis[k, 0, at, :] = value
        return carry

    lax.fori_loop(0, rows // 16, step, 0)


def shards(probes, weight, courant, upwind_flags):
    count, planes, rows, width = probes.shape
    sizes = tuple(lax.axis_size(axis) for axis in ("gz", "gy", "pa"))
    n_gz, n_gy, n_pa = sizes
    total = 2 * count
    team = n_gy * n_pa
    groups = count // GROUP
    f32 = jnp.float32
    dma = pltpu.SemaphoreType.DMA
    in_hbm = pl.BlockSpec(memory_space=pltpu.HBM)
    held = pl.BlockSpec(memory_space=pltpu.VMEM)
    y_own, y_part, fact = pl.pallas_call(
        functools.partial(sketch_kernel, sizes),
        out_shape=(
            pltpu.VMEM(probes.shape, f32),
            pltpu.VMEM(probes.shape, f32),
            pltpu.VMEM((total, 128), f32),
        ),
        in_specs=[in_hbm] * 4,
        out_specs=(held, held, held),
        scratch_shapes=[
            pltpu.VMEM((count, planes + 2, rows + 2 * PAD, width), f32),
            pltpu.VMEM((count, planes + 2, rows + 2 * PAD, width), f32),
            pltpu.VMEM(courant.shape, f32),
            pltpu.VMEM(upwind_flags.shape, jnp.int32),
            pltpu.VMEM(weight.shape, f32),
            pltpu.VMEM((2, planes, rows, width), f32),
            pltpu.VMEM((total * total, 8, 128), f32),
            pltpu.VMEM((total * total, 128), f32),
            pltpu.VMEM((total, 128), f32),
            pltpu.VMEM((team, total, 128), f32),
            pltpu.VMEM((total, 128), f32),
            pltpu.VMEM((n_gz, total, 128), f32),
            dma((4,)),
            dma((2, 2, groups)),
            dma((2, 2, groups)),
            dma((2, planes)),
            dma((2, planes)),
            dma((1 + 2 * groups,)),
            dma((1 + 2 * groups,)),
            dma((team,)),
            dma((team,)),
            dma((n_gz,)),
            dma((n_gz,)),
            dma((2, planes)),
            dma((2, planes)),
            dma((planes,)),
            dma((planes,)),
        ],
        compiler_params=pltpu.CompilerParams(
            collective_id=0, has_side_effects=True, vmem_limit_bytes=54 * 1024 * 1024),
        name="sketch",
    )(probes, weight, courant, upwind_flags)
    block = pl.BlockSpec((count, 1, rows, width), lambda z: (0, z, 0, 0))
    return pl.pallas_call(
        basis_kernel,
        grid=(planes,),
        out_shape=(
            jax.ShapeDtypeStruct(probes.shape, f32),
            jax.ShapeDtypeStruct((total, total), f32),
        ),
        in_specs=[
            pl.BlockSpec(memory_space=pltpu.SMEM),
            pl.BlockSpec((total, 128), lambda z: (0, 0)),
            held,
            held,
        ],
        out_specs=(block, pl.BlockSpec((total, total), lambda z: (0, 0))),
        compiler_params=pltpu.CompilerParams(vmem_limit_bytes=16 * 1024 * 1024),
        name="basis",
    )(fact, fact, y_own, y_part)


def solution(mesh):
    placed = (
        P("pa", "gz", "gy", None),
        P("gz", "gy", None),
        P(None, None, "gz", "gy", None),
        P(None, None, "gz", "gy", None),
    )
    return jax.shard_map(
        shards,
        mesh=mesh,
        in_specs=placed,
        out_specs=(P("pa", "gz", "gy", None), P()),
        check_vma=False,
    )
```
